256 devices in a mesh: dp: 32 (over y, z_hi, x), tensor: 8 (over z_lo, core).
Axes of the slice: x: 4, y: 4, z: 8 (z_hi: 2, z_lo: 4; z = z_hi * 4 + z_lo), core: 2. Of those that a mesh axis runs over, the one named last changes fastest.
Arguments:
- inputs: bfloat16 [32768, 1536], P(('dp', 'tensor')), may hold values from -360 to 360
- norm_gain: float32 [1536], replicated, may hold values from 0.1 to 1.9
- norm_bias: float32 [1536], replicated, may hold values from -3 to 3
- w_in: bfloat16 [1536, 6144], P('dp', 'tensor'), may hold values from -0.15625 to 0.15625
- bias_in: float32 [6144], P('tensor'), may hold values from -3 to 3
- w_out: bfloat16 [6144, 1536], P('tensor', 'dp'), may hold values from -0.078125 to 0.078125
- grad_out: bfloat16 [32768, 1536], P(('dp', 'tensor')), may hold values from -24 to 24
Outputs:
- grad_in: bfloat16 [32768, 1536], P(('dp', 'tensor'))
- grad_w_in: float32 [1536, 6144], P('dp', 'tensor')
- grad_w_out: float32 [6144, 1536], P('tensor', 'dp')
The draws below stay inside these ranges and needn't reach their ends.
All inputs are finite; a program needn't handle non-finite values.
Results may differ from the reference program's by a relative error of at most 0.0054.
Values may be sent and summed in bfloat16 or wider, within the bound.
No kernel may reach another device: no remote copies, remote signals or barrier semaphores. Data moves between devices by JAX's collectives and lax.ppermute only.
A program may use at most 128 MiB of HBM per device.

```python
import math
import jax
import jax.numpy as jnp
from jax import lax

D = 1536
FF = 6144
TOK_DEV = 128
TOKENS = 32768
N_DP = 32
N_TENSOR = 8


def draw_inputs(key, part):
    key = jax.random.fold_in(key, 11)
    keys = jax.random.split(key, 4)
    base = jnp.clip(jax.random.normal(keys[0], (TOKENS, D), jnp.float32), -4.0, 4.0)
    row_scale = jnp.exp(jax.random.uniform(keys[1], (TOKENS, 1), jnp.float32) * math.log(10.0))
    col_scale = jnp.exp(jax.random.uniform(keys[2], (1, D), jnp.float32) * math.log(3.0))
    pairing = jax.random.permutation(keys[3], N_DP)
    row_block = jnp.arange(TOKENS, dtype=jnp.int32) // (TOK_DEV * N_TENSOR)
    col_block = jnp.arange(D, dtype=jnp.int32) // (D // N_DP)
    spike = jnp.where(pairing[row_block][:, None] == col_block[None, :], 3.0, 1.0)
    return (base * row_scale * col_scale * spike).astype(jnp.bfloat16)


def spiked(entries, rng, source, target, parts, factor):
    def block_of(dim):
        return (jnp.arange(entries.shape[dim]) // (entries.shape[dim] // parts)).reshape((-1,) + (1,) * (entries.ndim - 1 - dim))

    one_side = jax.random.permutation(rng, parts)[block_of(target)]
    second = (block_of(target) + parts // 2) % parts
    return jnp.where((block_of(source) == one_side) | (block_of(source) == second), factor * entries, entries)


def shard_levels(stream_key, shape, cuts, low, high):
    level, own = 1.0, jax.random.fold_in(stream_key, 6)
    for axis_at, parts in cuts:
        steps = jnp.exp(jax.random.uniform(jax.random.fold_in(own, axis_at), (parts,), jnp.float32, low / len(cuts), high / len(cuts)))
        level = level * jnp.repeat(steps, shape[axis_at] // parts).reshape([-1 if axis == axis_at else 1 for axis in range(len(shape))])
    return level


def normal_values(rng, shape, spread, most, pieces=(), held_as=jnp.bfloat16):
    drawn = jax.random.normal(rng, shape, jnp.float32) * spread
    if len(pieces) > 0:
        drawn = shard_levels(rng, shape, pieces, -0.22, 0.18) * drawn
    return jnp.clip(drawn, min=-most, max=most).astype(held_as)


def heavy_noise(own_key, dims, width, most, shards, heavy, kind=jnp.bfloat16):
    drawn = width * jax.random.normal(own_key, dims, jnp.float32)
    if shards:
        drawn = drawn * shard_levels(own_key, dims, shards, -0.22, 0.18)
    return jnp.clip(spiked(drawn, jax.random.fold_in(own_key, 3), *heavy), -most, most).astype(kind)


def setup_inputs(seed: int = 0) -> dict:
    seeds = jax.random.split(jax.random.key(seed), 8)
    inputs = draw_inputs(jax.random.fold_in(seeds[7], 71), 0)
    norm_gain = jnp.clip(1.0 + 0.18 * jax.random.normal(seeds[1], (D,), jnp.float32), 0.1, 1.9)
    norm_bias = normal_values(seeds[2], (D,), 0.5, 3.0, (), jnp.float32)
    w_in = normal_values(seeds[3], (D, FF), D ** -0.5, 0.15625, ((0, 32), (1, 8)))
    bias_in = normal_values(seeds[4], (FF,), 0.5, 3.0, ((0, 8),), jnp.float32)
    w_out = normal_values(seeds[5], (FF, D), FF ** -0.5, 0.078125, ((0, 8), (1, 32)))
    grad_out = heavy_noise(seeds[6], (TOKENS, D), 1.0, 24.0, ((0, 256),), (0, 1, 256, 6.0))
    return dict(inputs=inputs, norm_gain=norm_gain, norm_bias=norm_bias, w_in=w_in, bias_in=bias_in, w_out=w_out, grad_out=grad_out)


def layer_rows(rows_in, norm_gain, norm_bias):
    centred = rows_in.astype(jnp.float32)
    centred = centred - lax.optimization_barrier(jnp.mean(centred, axis=-1, keepdims=True))
    variance = lax.optimization_barrier(jnp.mean(centred * centred, axis=-1, keepdims=True))
    inv_scale = lax.rsqrt(variance + 1e-05)
    normed = centred * inv_scale
    return (normed, inv_scale, (normed * norm_gain + norm_bias).astype(jnp.bfloat16))

def reference(inputs, norm_gain, norm_bias, w_in, bias_in, w_out, grad_out):
    block_rows = TOK_DEV * N_TENSOR
    blocks = TOKENS // block_rows
    frames = inputs.reshape(blocks, block_rows, D)
    grads = grad_out.reshape(blocks, block_rows, D)

    def block_step(carry, pair):
        sum_in, sum_out = carry
        rows_in, rows_grad = pair
        normed, inv_scale, normed_in = layer_rows(rows_in, norm_gain, norm_bias)
        pre_act = jnp.dot(normed_in, w_in, preferred_element_type=jnp.float32) + bias_in
        logistic = jax.nn.sigmoid(pre_act)
        activated = (pre_act * logistic).astype(jnp.bfloat16)
        grad_act = 0.5 * lax.dot_general(rows_grad, w_out, (((1,), (1,)), ((), ())), preferred_element_type=jnp.float32)
        grad_pre = (grad_act * logistic * (1.0 + pre_act * (1.0 - logistic))).astype(jnp.bfloat16)
        sum_out = sum_out + 0.5 * lax.dot_general(activated, rows_grad, (((0,), (0,)), ((), ())), preferred_element_type=jnp.float32)
        sum_in = sum_in + lax.dot_general(normed_in, grad_pre, (((0,), (0,)), ((), ())), preferred_element_type=jnp.float32)
        grad_normed = lax.dot_general(grad_pre, w_in, (((1,), (1,)), ((), ())), preferred_element_type=jnp.float32)
        scaled = grad_normed * norm_gain
        first = lax.optimization_barrier(jnp.mean(scaled, axis=-1, keepdims=True))
        second = lax.optimization_barrier(jnp.mean(scaled * normed, axis=-1, keepdims=True))
        result = rows_grad.astype(jnp.float32) + inv_scale * (scaled - first - normed * second)
        return ((sum_in, sum_out), result.astype(jnp.bfloat16))
    start_sums = (jnp.zeros((D, FF), jnp.float32), jnp.zeros((FF, D), jnp.float32))
    (grad_w_in, grad_w_out), grad_in = lax.scan(block_step, start_sums, (frames, grads))
    return (grad_in.reshape(TOKENS, D), grad_w_in, grad_w_out)
```

```python
import functools

import jax
import jax.numpy as jnp
from jax import lax
from jax.experimental import pallas as pl
from jax.experimental.pallas import tpu as pltpu
from jax.sharding import Mesh, PartitionSpec as P

D = 1536
FD = 768
TD = 128
RB = 48
BF = jnp.bfloat16
F32 = jnp.float32
Z = ("zh", "zl")
X_STEPS = (0, 1, -1, 2)
Y_STEPS = (0, 1, -1, 2)
Z_STEPS = (0, 1, -1, 2, -2, 3, -3, 4)
SIZES = {"y": 4, "x": 4, "c": 2, Z: 8}
ANY = pl.BlockSpec(memory_space=pl.ANY)
VM = pl.BlockSpec(memory_space=pltpu.VMEM)
SM = pl.BlockSpec(memory_space=pltpu.SMEM)
PARAMS = pltpu.CompilerParams(vmem_limit_bytes=44 * 1024 * 1024)


def shift(value, axis, by):
    n = SIZES[axis]
    return lax.ppermute(value, axis, [(i, (i + by) % n) for i in range(n)])


def turn(value):
    pairs = [(y * 4 + z, z * 4 + y) for y in range(4) for z in range(4)]
    return lax.ppermute(value, ("y", "zl"), pairs)


def row_block(z, x):
    return ((z % 4) * 8 + (z // 4) * 4 + x) * RB


def rows_at(ref, z, x):
    return ref.at[pl.ds(pl.multiple_of(row_block(z, x), 16), RB)]


def norm_kernel(x_ref, gain_ref, bias_ref, grad_ref, out_ref):
    centred = x_ref[...].astype(F32)
    centred = centred - jnp.mean(centred, axis=-1, keepdims=True)
    variance = jnp.mean(centred * centred, axis=-1, keepdims=True)
    normed = centred * lax.rsqrt(variance + 1e-05)
    out_ref[0] = (normed * gain_ref[...] + bias_ref[...]).astype(BF)
    out_ref[1] = grad_ref[...]


def token_copies(pieces, kind, dst, sems):
    return [
        pltpu.make_async_copy(piece.at[kind], dst.at[pl.ds(i * TD, TD)], sems.at[i])
        for i, piece in enumerate(pieces)
    ]


def win_copies(pieces, me, dst, sems):
    copies = []
    for i, xs in enumerate(X_STEPS):
        for j, zs in enumerate(Z_STEPS):
            at = rows_at(dst, (me[1] - zs + 8) % 8, (me[0] - xs + 4) % 4)
            copies.append(pltpu.make_async_copy(pieces[i].at[j], at, sems.at[i * 8 + j]))
    return copies


def act_kernel(me, *refs):
    toks, wins = refs[:8], refs[8:12]
    wo_in, bias_ref, gp_ref, dwo_ref = refs[12:16]
    n_s, g_s, win_s, wo_s, dwo_s, sem_n, sem_g, sem_i, sem_o = refs[16:]
    n_copies = token_copies(toks, 0, n_s, sem_n)
    g_copies = token_copies(toks, 1, g_s, sem_g)
    i_copies = win_copies(wins, me, win_s, sem_i)
    o_copies = []
    for z in range(8):
        for i, xs in enumerate(X_STEPS):
            at = rows_at(wo_s, z, (me[0] - xs + 4) % 4)
            o_copies.append(pltpu.make_async_copy(wo_in.at[z, i], at, sem_o.at[z * 4 + i]))
    for group in (n_copies, i_copies, g_copies, o_copies):
        for copy in group:
            copy.start()
    for group in (n_copies, i_copies, g_copies, o_copies):
        for copy in group:
            copy.wait()

    def step(j, carry):
        cols = pl.ds(pl.multiple_of(j * 256, 256), 256)
        pre = jnp.dot(n_s[...], win_s[:, cols], preferred_element_type=F32) + bias_ref[:, cols]
        ga = 0.5 * jnp.dot(g_s[...], wo_s[:, cols], preferred_element_type=F32)
        s = jax.nn.sigmoid(pre)
        act = (pre * s).astype(BF)
        gp_ref[:, cols] = (ga * s * (1.0 + pre * (1.0 - s))).astype(BF)
        dwo = lax.dot_general(g_s[...], act, (((0,), (0,)), ((), ())), preferred_element_type=F32)
        dwo_s[:, cols] = (0.5 * dwo).astype(BF)
        return carry

    lax.fori_loop(0, 3, step, 0)
    outs = []
    for z in range(8):
        for i, xs in enumerate(X_STEPS):
            src = rows_at(dwo_s, z, (me[0] + xs + 4) % 4)
            outs.append(pltpu.make_async_copy(src, dwo_ref.at[z, i], sem_o.at[z * 4 + i]))
    for copy in outs:
        copy.start()
    for copy in outs:
        copy.wait()


def dwin_kernel(me, *refs):
    toks, gp_ref, outs = refs[:8], refs[8], refs[9:13]
    n_s, dw_s, sem_n, sem_o = refs[13:]
    copies = token_copies(toks, 0, n_s, sem_n)
    for copy in copies:
        copy.start()
    for copy in copies:
        copy.wait()

    def step(j, carry):
        cols = pl.ds(pl.multiple_of(j * 256, 256), 256)
        dw = lax.dot_general(
            n_s[...], gp_ref[:, cols], (((0,), (0,)), ((), ())), preferred_element_type=F32
        )
        dw_s[:, cols] = dw.astype(BF)
        return carry

    lax.fori_loop(0, 3, step, 0)
    copies = []
    for i, xs in enumerate(X_STEPS):
        for j, zs in enumerate(Z_STEPS):
            src = rows_at(dw_s, (me[1] + zs + 8) % 8, (me[0] + xs + 4) % 4)
            copies.append(pltpu.make_async_copy(src, outs[i].at[j], sem_o.at[i * 8 + j]))
    for copy in copies:
        copy.start()
    for copy in copies:
        copy.wait()


def dx_kernel(me, *refs):
    gp_ref, wins, own_ref, other_ref = refs[0], refs[1:5], refs[5], refs[6]
    win_s, sem_i = refs[7:]
    copies = win_copies(wins, me, win_s, sem_i)
    for copy in copies:
        copy.start()
    for copy in copies:
        copy.wait()

    def step(j, carry):
        cols = pl.ds(pl.multiple_of(j * 256, 256), 256)
        dx = lax.dot_general(
            gp_ref[...], win_s[cols, :], (((1,), (1,)), ((), ())), preferred_element_type=F32
        ).astype(BF)
        own_ref[:, cols] = dx[:512]
        other_ref[:, cols] = dx[512:]
        return carry

    lax.fori_loop(0, 6, step, 0)


def final_kernel(x_ref, gain_ref, grad_ref, a_ref, b_ref, c_ref, d_ref, out_ref):
    centred = x_ref[...].astype(F32)
    centred = centred - jnp.mean(centred, axis=-1, keepdims=True)
    variance = jnp.mean(centred * centred, axis=-1, keepdims=True)
    inv_scale = lax.rsqrt(variance + 1e-05)
    normed = centred * inv_scale
    total = (a_ref[...].astype(F32) + b_ref[...].astype(F32)) + (
        c_ref[...].astype(F32) + d_ref[...].astype(F32)
    )
    scaled = total * gain_ref[...]
    first = jnp.mean(scaled, axis=-1, keepdims=True)
    second = jnp.mean(scaled * normed, axis=-1, keepdims=True)
    result = grad_ref[...].astype(F32) + inv_scale * (scaled - first - normed * second)
    out_ref[...] = result.astype(BF)


def cost(flops, moved):
    return pl.CostEstimate(flops=flops, bytes_accessed=moved, transcendentals=0)


def add_up(parts):
    total = parts[0].astype(F32)
    for part in parts[1:]:
        total = total + part.astype(F32)
    return total


def on_device(inputs, norm_gain, norm_bias, w_in, bias_in, w_out, grad_out):
    me = jnp.stack([lax.axis_index("x"), lax.axis_index(Z)]).astype(jnp.int32)
    gain, nbias = norm_gain.reshape(1, D), norm_bias.reshape(1, D)

    wo_own = turn(w_out.T)
    win_own = turn(w_in)
    bias = turn(bias_in).reshape(1, FD)

    tok = pl.pallas_call(
        norm_kernel,
        out_shape=jax.ShapeDtypeStruct((2, TD, D), BF),
        in_specs=[VM] * 4,
        out_specs=VM,
        compiler_params=PARAMS,
        cost_estimate=cost(10 * TD * D, 8 * TD * D),
    )(inputs, gain, nbias, grad_out)

    wo_x = jnp.stack([wo_own] + [shift(wo_own, "x", s) for s in X_STEPS[1:]])
    wo_all = lax.all_gather(wo_x, Z, axis=0, tiled=False)

    own = [tok] + [shift(tok, "y", s) for s in Y_STEPS[1:]]
    toks = own + [shift(piece, "c", 1) for piece in own]

    win_z = jnp.stack([win_own] + [shift(win_own, Z, s) for s in Z_STEPS[1:]])
    wins = [win_z] + [shift(win_z, "x", s) for s in X_STEPS[1:]]

    mm = 2 * 1024 * FD * D
    gp, dwo = pl.pallas_call(
        act_kernel,
        out_shape=(
            jax.ShapeDtypeStruct((1024, FD), BF),
            jax.ShapeDtypeStruct((8, 4, RB, FD), BF),
        ),
        in_specs=[SM] + [ANY] * 13 + [VM],
        out_specs=(VM, ANY),
        scratch_shapes=[
            pltpu.VMEM((1024, D), BF),
            pltpu.VMEM((1024, D), BF),
            pltpu.VMEM((D, FD), BF),
            pltpu.VMEM((D, FD), BF),
            pltpu.VMEM((D, FD), BF),
            pltpu.SemaphoreType.DMA((8,)),
            pltpu.SemaphoreType.DMA((8,)),
            pltpu.SemaphoreType.DMA((32,)),
            pltpu.SemaphoreType.DMA((32,)),
        ],
        compiler_params=PARAMS,
        cost_estimate=cost(3 * mm, 16 << 20),
    )(me, *toks, *wins, wo_all, bias)

    dwo_z = lax.psum_scatter(dwo, Z, scatter_dimension=0, tiled=False)

    dws = pl.pallas_call(
        dwin_kernel,
        out_shape=[jax.ShapeDtypeStruct((8, RB, FD), BF)] * 4,
        in_specs=[SM] + [ANY] * 8 + [VM],
        out_specs=[ANY] * 4,
        scratch_shapes=[
            pltpu.VMEM((1024, D), BF),
            pltpu.VMEM((D, FD), BF),
            pltpu.SemaphoreType.DMA((8,)),
            pltpu.SemaphoreType.DMA((32,)),
        ],
        compiler_params=PARAMS,
        cost_estimate=cost(mm, 7 << 20),
    )(me, *toks, gp)

    dx_own, dx_other = pl.pallas_call(
        dx_kernel,
        out_shape=[jax.ShapeDtypeStruct((512, D), BF)] * 2,
        in_specs=[SM, VM] + [ANY] * 4,
        out_specs=[VM, VM],
        scratch_shapes=[pltpu.VMEM((D, FD), BF), pltpu.SemaphoreType.DMA((32,))],
        compiler_params=PARAMS,
        cost_estimate=cost(mm, 7 << 20),
    )(me, gp, *wins)

    dwin_x = add_up([dws[0]] + [shift(dws[i], "x", X_STEPS[i]) for i in range(1, 4)]).astype(BF)

    dx_swapped = shift(dx_other, "c", 1)
    parts = []
    for i, s in enumerate(Y_STEPS):
        rows = slice(i * TD, (i + 1) * TD)
        part = add_up([dx_own[rows], dx_swapped[rows]]).astype(BF)
        parts.append(part if i == 0 else shift(part, "y", -s))

    dwin = add_up([dwin_x[0]] + [shift(dwin_x[j], Z, Z_STEPS[j]) for j in range(1, 8)]).astype(BF)
    grad_w_in = turn(dwin).astype(F32)

    dwo_sum = add_up([dwo_z[0]] + [shift(dwo_z[i], "x", X_STEPS[i]) for i in range(1, 4)]).astype(BF)
    grad_w_out = turn(dwo_sum).astype(F32).T

    grad_in = pl.pallas_call(
        final_kernel,
        out_shape=jax.ShapeDtypeStruct((TD, D), BF),
        in_specs=[VM] * 7,
        out_specs=VM,
        compiler_params=PARAMS,
        cost_estimate=cost(20 * TD * D, 14 * TD * D),
    )(inputs, gain, grad_out, *parts)
    return grad_in, grad_w_in, grad_w_out


def solution(mesh):
    fine = Mesh(mesh.devices.reshape(4, 2, 4, 4, 2), ("y", "zh", "x", "zl", "c"))
    dp, tensor = ("y", "zh", "x"), ("zl", "c")
    rows = P(dp + tensor, None)
    return jax.shard_map(
        on_device,
        mesh=fine,
        in_specs=(rows, P(), P(), P(dp, tensor), P(tensor), P(tensor, dp), rows),
        out_specs=(rows, P(dp, tensor), P(tensor, dp)),
        check_vma=False,
    )
```

```python
import functools

import jax
import jax.numpy as jnp
from jax import lax
from jax.experimental import pallas as pl
from jax.experimental.pallas import tpu as pltpu
from jax.sharding import Mesh, PartitionSpec as P

D = 1536
FD = 768
TD = 128
RB = 48
BF = jnp.bfloat16
F32 = jnp.float32
Z = ("zh", "zl")
X_STEPS = (0, 1, -1, 2)
Z_STEPS = tuple((r, h) for r in (0, 1, -1, 2) for h in (0, 4))
RING = tuple((k, (0, 1, 2, 3)) for k in (0, -1, 1, -2, 2, -3, 3)) + ((-4, (0, 1)), (4, (2, 3)))
SIZES = {"y": 4, "x": 4, "c": 2, Z: 8}
ANY = pl.BlockSpec(memory_space=pl.ANY)
VM = pl.BlockSpec(memory_space=pltpu.VMEM)
SM = pl.BlockSpec(memory_space=pltpu.SMEM)
PARAMS = pltpu.CompilerParams(vmem_limit_bytes=60 * 1024 * 1024)


def shift(value, axis, by):
    n = SIZES[axis]
    return lax.ppermute(value, axis, [(i, (i + by) % n) for i in range(n)])


def turn(value):
    pairs = [(y * 4 + z, z * 4 + y) for y in range(4) for z in range(4)]
    return lax.ppermute(value, ("y", "zl"), pairs)


def row_block(z, x):
    return ((z % 4) * 8 + (z // 4) * 4 + x) * RB


def rows_at(ref, z, x):
    return ref.at[pl.ds(pl.multiple_of(row_block(z, x), 16), RB)]


def norm_kernel(x_ref, gain_ref, bias_ref, grad_ref, out_ref):
    centred = x_ref[...].astype(F32)
    centred = centred - jnp.mean(centred, axis=-1, keepdims=True)
    variance = jnp.mean(centred * centred, axis=-1, keepdims=True)
    normed = centred * lax.rsqrt(variance + 1e-05)
    out_ref[0] = (normed * gain_ref[...] + bias_ref[...]).astype(BF)
    out_ref[1] = grad_ref[...]


def token_copies(toks, me, kind, dst, sems):
    copies = []
    for i in range(8):
        owner = (i % 4) * 2 + (me[2] if i < 4 else 1 - me[2])
        at = dst.at[pl.ds(i * TD, TD)]
        copies.append(pltpu.make_async_copy(toks.at[owner, kind], at, sems.at[i]))
    return copies


def win_copies(pieces, me, dst, sems):
    copies = []
    for i in range(4):
        for j, (r, h) in enumerate(Z_STEPS):
            at = rows_at(dst, (me[1] - r + h + 8) % 8, i)
            copies.append(pltpu.make_async_copy(pieces.at[i, j], at, sems.at[i * 8 + j]))
    return copies


def main_kernel(me, *refs):
    toks, wins, wos = refs[0], refs[1], refs[2:11]
    bias_ref, gp_ref, dwo_ref, dwin_ref = refs[11:15]
    n_s, g_s, win_s, wo_s, act_s, dwo_s, dwin_s, sem_n, sem_g, sem_i, sem_o = refs[15:]
    n_copies = token_copies(toks, me, 0, n_s, sem_n)
    g_copies = token_copies(toks, me, 1, g_s, sem_g)
    i_copies = win_copies(wins, me, win_s, sem_i)
    o_copies = []
    for piece, (away, xs) in zip(wos, RING):
        for k, i in enumerate(xs):
            at = rows_at(wo_s, (me[1] + away + 8) % 8, (me[0] - X_STEPS[i] + 4) % 4)
            o_copies.append(pltpu.make_async_copy(piece.at[k], at, sem_o.at[len(o_copies)]))
    for copy in n_copies + i_copies + g_copies + o_copies:
        copy.start()
    for copy in n_copies + i_copies + g_copies + o_copies:
        copy.wait()

    def hidden(j, carry):
        cols = pl.ds(pl.multiple_of(j * 256, 256), 256)
        pre = jnp.dot(n_s[...], win_s[:, cols], preferred_element_type=F32) + bias_ref[:, cols]
        ga = 0.5 * jnp.dot(g_s[...], wo_s[:, cols], preferred_element_type=F32)
        s = jax.nn.sigmoid(pre)
        act_s[:, cols] = (pre * s).astype(BF)
        gp_ref[:, cols] = (ga * s * (1.0 + pre * (1.0 - s))).astype(BF)
        return carry

    lax.fori_loop(0, 3, hidden, 0)
    dims = (((0,), (0,)), ((), ()))

    def out_grad(zl, carry):
        rows = pl.ds(pl.multiple_of(zl * 384, 384), 384)
        dwo = lax.dot_general(g_s[:, rows], act_s[...], dims, preferred_element_type=F32)
        dwo_s[rows, :] = (0.5 * dwo).astype(BF)
        for zh in range(2):
            for i, xs in enumerate(X_STEPS):
                src = rows_at(dwo_s, zh * 4 + zl, (me[0] + xs + 4) % 4)
                dst = dwo_ref.at[zh * 4 + zl, i]
                pltpu.make_async_copy(src, dst, sem_o.at[zl * 8 + zh * 4 + i]).start()
        return carry

    def in_grad(zl, carry):
        rows = pl.ds(pl.multiple_of(zl * 384, 384), 384)
        dwin = lax.dot_general(n_s[:, rows], gp_ref[...], dims, preferred_element_type=F32)
        dwin_s[rows, :] = dwin.astype(BF)
        for zh in range(2):
            away = (zh * 4 + zl - me[1] + 8) % 8
            quarter = away % 4
            place = 2 * (quarter ^ (quarter // 2)) + ((away + 1) // 4) % 2
            for x in range(4):
                src = rows_at(dwin_s, zh * 4 + zl, x)
                dst = dwin_ref.at[x, place]
                pltpu.make_async_copy(src, dst, sem_i.at[zl * 8 + zh * 4 + x]).start()
        return carry

    lax.fori_loop(0, 4, out_grad, 0)
    lax.fori_loop(0, 4, in_grad, 0)
    for k in range(32):
        pltpu.make_async_copy(dwo_s.at[pl.ds(0, RB)], dwo_ref.at[0, 0], sem_o.at[k]).wait()
        pltpu.make_async_copy(dwin_s.at[pl.ds(0, RB)], dwin_ref.at[0, 0], sem_i.at[k]).wait()


def dx_kernel(me, *refs):
    gp_ref, wins, outs = refs[0], refs[1], refs[3:5]
    win_s, sem_i = refs[5:]
    copies = win_copies(wins, me, win_s, sem_i)
    for copy in copies:
        copy.start()
    for copy in copies:
        copy.wait()

    def step(j, carry):
        cols = pl.ds(pl.multiple_of(j * 512, 512), 512)
        dx = lax.dot_general(
            gp_ref[...], win_s[cols, :], (((1,), (1,)), ((), ())), preferred_element_type=F32
        ).astype(BF)
        outs[0][:, cols] = dx[:512]
        outs[1][:, cols] = dx[512:]
        return carry

    lax.fori_loop(0, 3, step, 0)


def final_kernel(x_ref, gain_ref, grad_ref, dx_ref, out_ref):
    centred = x_ref[...].astype(F32)
    centred = centred - jnp.mean(centred, axis=-1, keepdims=True)
    variance = jnp.mean(centred * centred, axis=-1, keepdims=True)
    inv_scale = lax.rsqrt(variance + 1e-05)
    normed = centred * inv_scale
    total = add_up([dx_ref[i] for i in range(4)])
    scaled = total * gain_ref[...]
    first = jnp.mean(scaled, axis=-1, keepdims=True)
    second = jnp.mean(scaled * normed, axis=-1, keepdims=True)
    result = grad_ref[...].astype(F32) + inv_scale * (scaled - first - normed * second)
    out_ref[...] = result.astype(BF)


def cost(flops, moved):
    return pl.CostEstimate(flops=flops, bytes_accessed=moved, transcendentals=0)


def add_up(parts):
    total = parts[0].astype(F32)
    for part in parts[1:]:
        total = total + part.astype(F32)
    return total


def on_device(inputs, norm_gain, norm_bias, w_in, bias_in, w_out, grad_out):
    me = jnp.stack([lax.axis_index(a) for a in ("x", Z, "c")]).astype(jnp.int32)

    wo_own = turn(w_out.T)
    win_own = turn(w_in)
    bias = turn(bias_in).reshape(1, FD)
    tok = pl.pallas_call(
        norm_kernel,
        out_shape=jax.ShapeDtypeStruct((2, TD, D), BF),
        in_specs=[VM] * 4,
        out_specs=VM,
        compiler_params=PARAMS,
        cost_estimate=cost(10 * TD * D, 8 * TD * D),
    )(inputs, norm_gain, norm_bias, grad_out)

    wo_own, win_own, tok = lax.optimization_barrier((wo_own, win_own, tok))
    wo_x = [wo_own] + [shift(wo_own, "x", s) for s in X_STEPS[1:]]
    win_far = shift(win_own, Z, 4)
    *wo_x, win_far = lax.optimization_barrier((*wo_x, win_far))
    toks = lax.all_gather(tok, ("y", "c"), axis=0, tiled=False)

    win_h = jnp.stack([win_own, win_far])
    win_z = [win_h] + [shift(win_h, Z, r) for r in (1, -1, 2)]
    wo_h = jnp.stack(wo_x)
    ahead, back = shift(wo_h, Z, 1), shift(wo_h, Z, -1)
    ahead, back, *win_z = lax.optimization_barrier((ahead, back, *win_z))
    win_z = jnp.broadcast_to(jnp.concatenate(win_z)[None], (4, 8, RB, FD))
    wins = lax.all_to_all(win_z, "x", 0, 0, tiled=True)
    wos = [wo_h, ahead, back]
    for _ in range(2):
        ahead, back = shift(ahead, Z, 1), shift(back, Z, -1)
        wos += [ahead, back]
    wos += [shift(ahead[:2], Z, 1), shift(back[2:], Z, -1)]

    mm = 2 * 1024 * FD * D
    gp, dwo, dws = pl.pallas_call(
        main_kernel,
        out_shape=(
            jax.ShapeDtypeStruct((1024, FD), BF),
            jax.ShapeDtypeStruct((8, 4, RB, FD), BF),
            jax.ShapeDtypeStruct((4, 8, RB, FD), BF),
        ),
        in_specs=[SM] + [ANY] * 11 + [VM],
        out_specs=(VM, ANY, ANY),
        scratch_shapes=[
            pltpu.VMEM((1024, D), BF),
            pltpu.VMEM((1024, D), BF),
            pltpu.VMEM((D, FD), BF),
            pltpu.VMEM((D, FD), BF),
            pltpu.VMEM((1024, FD), BF),
            pltpu.VMEM((D, FD), BF),
            pltpu.VMEM((D, FD), BF),
            pltpu.SemaphoreType.DMA((8,)),
            pltpu.SemaphoreType.DMA((8,)),
            pltpu.SemaphoreType.DMA((32,)),
            pltpu.SemaphoreType.DMA((32,)),
        ],
        compiler_params=PARAMS,
        cost_estimate=cost(4 * mm, 20 << 20),
    )(me, toks, wins, *wos, bias)

    dwo_z = lax.psum_scatter(dwo, Z, scatter_dimension=0, tiled=False)
    note = shift(dws[0, 0, :16], "c", 1)
    dx_own, dx_other = pl.pallas_call(
        dx_kernel,
        out_shape=[jax.ShapeDtypeStruct((512, D), BF)] * 2,
        in_specs=[SM, VM] + [ANY] * 2,
        out_specs=[VM] * 2,
        scratch_shapes=[pltpu.VMEM((D, FD), BF), pltpu.SemaphoreType.DMA((32,))],
        compiler_params=PARAMS,
        cost_estimate=cost(mm, 7 << 20),
    )(me, gp, wins, note)

    dws = lax.all_to_all(dws, "x", 0, 0, tiled=True)
    dx_c = add_up([dx_own, shift(dx_other, "c", 1)]).astype(BF)
    dx_y = lax.all_to_all(dx_c, "y", 0, 0, tiled=True).reshape(4, TD, D)
    dwin_x = add_up([dws[i] for i in range(4)]).astype(BF)
    pairs = [dwin_x[2 * i : 2 * i + 2] for i in range(4)]
    dwin_z = add_up([pairs[0]] + [shift(pairs[i], Z, r) for i, r in ((1, 1), (2, -1), (3, 2))]).astype(BF)
    dwin = add_up([dwin_z[0], shift(dwin_z[1], Z, 4)]).astype(BF)
    grad_w_in = turn(dwin).astype(F32)

    dwo_sum = add_up([dwo_z[0]] + [shift(dwo_z[i], "x", X_STEPS[i]) for i in range(1, 4)]).astype(BF)
    grad_w_out = turn(dwo_sum).astype(F32).T

    grad_in = pl.pallas_call(
        final_kernel,
        out_shape=jax.ShapeDtypeStruct((TD, D), BF),
        in_specs=[VM] * 4,
        out_specs=VM,
        compiler_params=PARAMS,
        cost_estimate=cost(20 * TD * D, 14 * TD * D),
    )(inputs, norm_gain, grad_out, dx_y)
    return grad_in, grad_w_in, grad_w_out


def solution(mesh):
    fine = Mesh(mesh.devices.reshape(4, 2, 4, 4, 2), ("y", "zh", "x", "zl", "c"))
    dp, tensor = ("y", "zh", "x"), ("zl", "c")
    rows = P(dp + tensor, None)
    return jax.shard_map(
        on_device,
        mesh=fine,
        in_specs=(rows, P(), P(), P(dp, tensor), P(tensor), P(tensor, dp), rows),
        out_specs=(rows, P(dp, tensor), P(tensor, dp)),
        check_vma=False,
    )
```

```python
import functools

import jax
import jax.numpy as jnp
from jax import lax
from jax.experimental import pallas as pl
from jax.experimental.pallas import tpu as pltpu
from jax.sharding import Mesh, PartitionSpec as P

D = 1536
FD = 768
TD = 128
RB = 48
BF = jnp.bfloat16
F32 = jnp.float32
Z = ("zh", "zl")
X_STEPS = (0, 1, -1, 2)
Z_STEPS = tuple((r, h) for r in (0, 1, -1, 2) for h in (0, 4))
RING = tuple((k, (0, 1, 2, 3)) for k in (0, -1, 1, -2, 2, -3, 3)) + ((-4, (0, 1)), (4, (2, 3)))
SIZES = {"y": 4, "x": 4, "c": 2, Z: 8}
ANY = pl.BlockSpec(memory_space=pl.ANY)
VM = pl.BlockSpec(memory_space=pltpu.VMEM)
SM = pl.BlockSpec(memory_space=pltpu.SMEM)
PARAMS = pltpu.CompilerParams(vmem_limit_bytes=60 * 1024 * 1024)


def shift(value, axis, by):
    n = SIZES[axis]
    return lax.ppermute(value, axis, [(i, (i + by) % n) for i in range(n)])


def turn(value, far=0):
    pairs = [
        (y * 8 + h * 4 + z, z * 8 + (h ^ far) * 4 + y)
        for y in range(4)
        for h in range(2)
        for z in range(4)
    ]
    return lax.ppermute(value, ("y", "zh", "zl"), pairs)


def row_block(z, x):
    return ((z % 4) * 8 + (z // 4) * 4 + x) * RB


def rows_at(ref, z, x):
    return ref.at[pl.ds(pl.multiple_of(row_block(z, x), 16), RB)]


def norm_kernel(x_ref, gain_ref, bias_ref, grad_ref, out_ref):
    centred = x_ref[...].astype(F32)
    centred = centred - jnp.mean(centred, axis=-1, keepdims=True)
    variance = jnp.mean(centred * centred, axis=-1, keepdims=True)
    normed = centred * lax.rsqrt(variance + 1e-05)
    out_ref[0] = (normed * gain_ref[...] + bias_ref[...]).astype(BF)
    out_ref[1] = grad_ref[...]


def token_copies(toks, me, kind, dst, sems):
    copies = []
    for i in range(8):
        owner = (i % 4) * 2 + (me[2] if i < 4 else 1 - me[2])
        at = dst.at[pl.ds(i * TD, TD)]
        copies.append(pltpu.make_async_copy(toks.at[owner, kind], at, sems.at[i]))
    return copies


def win_copies(pieces, me, dst, sems):
    copies = []
    for i in range(4):
        for j, (r, h) in enumerate(Z_STEPS):
            at = rows_at(dst, (me[1] - r + h + 8) % 8, i)
            copies.append(pltpu.make_async_copy(pieces.at[i, j], at, sems.at[i * 8 + j]))
    return copies


def main_kernel(me, *refs):
    toks, wins, wos = refs[0], refs[1], refs[2:11]
    bias_ref, gp_ref, dwo_ref = refs[11:14]
    n_s, g_s, win_s, wo_s, act_s, dwo_s, sem_n, sem_g, sem_i, sem_o = refs[14:]
    n_copies = token_copies(toks, me, 0, n_s, sem_n)
    g_copies = token_copies(toks, me, 1, g_s, sem_g)
    i_copies = win_copies(wins, me, win_s, sem_i)
    o_copies = []
    for piece, (away, xs) in zip(wos, RING):
        for k, i in enumerate(xs):
            at = rows_at(wo_s, (me[1] + away + 8) % 8, (me[0] - X_STEPS[i] + 4) % 4)
            o_copies.append(pltpu.make_async_copy(piece.at[k], at, sem_o.at[len(o_copies)]))
    for copy in n_copies + i_copies + g_copies + o_copies:
        copy.start()
    for copy in n_copies + i_copies + g_copies + o_copies:
        copy.wait()

    def hidden(j, carry):
        cols = pl.ds(pl.multiple_of(j * 256, 256), 256)
        pre = jnp.dot(n_s[...], win_s[:, cols], preferred_element_type=F32) + bias_ref[:, cols]
        ga = 0.5 * jnp.dot(g_s[...], wo_s[:, cols], preferred_element_type=F32)
        s = jax.nn.sigmoid(pre)
        act_s[:, cols] = (pre * s).astype(BF)
        gp_ref[:, cols] = (ga * s * (1.0 + pre * (1.0 - s))).astype(BF)
        return carry

    lax.fori_loop(0, 3, hidden, 0)
    dims = (((0,), (0,)), ((), ()))

    def out_grad(zl, carry):
        rows = pl.ds(pl.multiple_of(zl * 384, 384), 384)
        dwo = lax.dot_general(g_s[:, rows], act_s[...], dims, preferred_element_type=F32)
        dwo_s[rows, :] = (0.5 * dwo).astype(BF)
        for zh in range(2):
            for i, xs in enumerate(X_STEPS):
                src = rows_at(dwo_s, zh * 4 + zl, (me[0] + xs + 4) % 4)
                dst = dwo_ref.at[zh * 4 + zl, i]
                pltpu.make_async_copy(src, dst, sem_o.at[zl * 8 + zh * 4 + i]).start()
        return carry

    lax.fori_loop(0, 4, out_grad, 0)
    for k in range(32):
        pltpu.make_async_copy(dwo_s.at[pl.ds(0, RB)], dwo_ref.at[0, 0], sem_o.at[k]).wait()


def dwin_kernel(me, *refs):
    toks, gp_ref, dwin_ref, n_s, dwin_s, sem_n, sem_i = refs
    copies = token_copies(toks, me, 0, n_s, sem_n)
    for copy in copies:
        copy.start()
    for copy in copies:
        copy.wait()

    def in_grad(zl, carry):
        rows = pl.ds(pl.multiple_of(zl * 384, 384), 384)
        dims = (((0,), (0,)), ((), ()))
        dwin = lax.dot_general(n_s[:, rows], gp_ref[...], dims, preferred_element_type=F32)
        dwin_s[rows, :] = dwin.astype(BF)
        for zh in range(2):
            away = (zh * 4 + zl - me[1] + 8) % 8
            quarter = away % 4
            place = 2 * (quarter ^ (quarter // 2)) + ((away + 1) // 4) % 2
            for x in range(4):
                src = rows_at(dwin_s, zh * 4 + zl, x)
                dst = dwin_ref.at[x, place]
                pltpu.make_async_copy(src, dst, sem_i.at[zl * 8 + zh * 4 + x]).start()
        return carry

    lax.fori_loop(0, 4, in_grad, 0)
    for k in range(32):
        pltpu.make_async_copy(dwin_s.at[pl.ds(0, RB)], dwin_ref.at[0, 0], sem_i.at[k]).wait()


def dx_kernel(me, *refs):
    gp_ref, wins, outs = refs[0], refs[1], refs[3:6]
    win_s, sem_i = refs[6:]
    copies = win_copies(wins, me, win_s, sem_i)
    for copy in copies:
        copy.start()
    for copy in copies:
        copy.wait()

    def step(j, carry):
        cols = pl.ds(pl.multiple_of(j * 512, 512), 512)
        dx = lax.dot_general(
            gp_ref[...], win_s[cols, :], (((1,), (1,)), ((), ())), preferred_element_type=F32
        ).astype(BF)
        outs[0][:, cols] = dx[:512]
        for i in range(2):
            outs[1 + i][:, cols] = dx[512 + 256 * i : 512 + 256 * (i + 1)]
        return carry

    lax.fori_loop(0, 3, step, 0)


def final_kernel(x_ref, gain_ref, grad_ref, dx_ref, after_ref, out_ref):
    centred = x_ref[...].astype(F32)
    centred = centred - jnp.mean(centred, axis=-1, keepdims=True)
    variance = jnp.mean(centred * centred, axis=-1, keepdims=True)
    inv_scale = lax.rsqrt(variance + 1e-05)
    normed = centred * inv_scale
    total = add_up([dx_ref[i] for i in range(4)])
    scaled = total * gain_ref[...]
    first = jnp.mean(scaled, axis=-1, keepdims=True)
    second = jnp.mean(scaled * normed, axis=-1, keepdims=True)
    result = grad_ref[...].astype(F32) + inv_scale * (scaled - first - normed * second)
    out_ref[...] = result.astype(BF)


def cost(flops, moved):
    return pl.CostEstimate(flops=flops, bytes_accessed=moved, transcendentals=0)


def add_up(parts):
    total = parts[0].astype(F32)
    for part in parts[1:]:
        total = total + part.astype(F32)
    return total


def on_device(inputs, norm_gain, norm_bias, w_in, bias_in, w_out, grad_out):
    me = jnp.stack([lax.axis_index(a) for a in ("x", Z, "c")]).astype(jnp.int32)

    both = turn(jnp.stack([w_in, w_out.T]))
    win_far = turn(w_in, 1)
    bias = turn(bias_in)

    tok = pl.pallas_call(
        norm_kernel,
        out_shape=jax.ShapeDtypeStruct((2, TD, D), BF),
        in_specs=[VM] * 4,
        out_specs=VM,
        compiler_params=PARAMS,
        cost_estimate=cost(10 * TD * D, 8 * TD * D),
    )(inputs, norm_gain, norm_bias, grad_out)

    me, bias, both, win_far, tok = lax.optimization_barrier((me, bias, both, win_far, tok))
    toks = lax.all_gather(tok, ("y", "c"), axis=0, tiled=False)

    wo_x = [both[1]] + [shift(both[1], "x", s) for s in X_STEPS[1:]]
    win_h = jnp.stack([both[0], win_far])
    win_z = [win_h] + [shift(win_h, Z, r) for r in (1, -1, 2)]
    *wo_x, w0, w1, w2, w3 = lax.optimization_barrier((*wo_x, *win_z))
    win_z = [w0, w1, w2, w3]
    wo_h = jnp.stack(wo_x)
    ahead, back = shift(wo_h, Z, 1), shift(wo_h, Z, -1)
    win_z = jnp.broadcast_to(jnp.concatenate(win_z)[None], (4, 8, RB, FD))
    wins = lax.all_to_all(win_z, "x", 0, 0, tiled=True)
    wos = [wo_h, ahead, back]
    for _ in range(2):
        ahead, back = shift(ahead, Z, 1), shift(back, Z, -1)
        wos += [ahead, back]
    wos += [shift(ahead[:2], Z, 1), shift(back[2:], Z, -1)]
    bias = bias.reshape(1, FD)

    mm = 2 * 1024 * FD * D
    gp, dwo = pl.pallas_call(
        main_kernel,
        out_shape=(
            jax.ShapeDtypeStruct((1024, FD), BF),
            jax.ShapeDtypeStruct((8, 4, RB, FD), BF),
        ),
        in_specs=[SM] + [ANY] * 11 + [VM],
        out_specs=(VM, ANY),
        scratch_shapes=[
            pltpu.VMEM((1024, D), BF),
            pltpu.VMEM((1024, D), BF),
            pltpu.VMEM((D, FD), BF),
            pltpu.VMEM((D, FD), BF),
            pltpu.VMEM((1024, FD), BF),
            pltpu.VMEM((D, FD), BF),
            pltpu.SemaphoreType.DMA((8,)),
            pltpu.SemaphoreType.DMA((8,)),
            pltpu.SemaphoreType.DMA((32,)),
            pltpu.SemaphoreType.DMA((32,)),
        ],
        compiler_params=PARAMS,
        cost_estimate=cost(3 * mm, 20 << 20),
    )(me, toks, wins, *wos, bias)

    dwo_z = lax.psum_scatter(dwo, Z, scatter_dimension=0, tiled=False)

    dws = pl.pallas_call(
        dwin_kernel,
        out_shape=jax.ShapeDtypeStruct((4, 8, RB, FD), BF),
        in_specs=[SM, ANY, VM],
        out_specs=ANY,
        scratch_shapes=[
            pltpu.VMEM((1024, D), BF),
            pltpu.VMEM((D, FD), BF),
            pltpu.SemaphoreType.DMA((8,)),
            pltpu.SemaphoreType.DMA((32,)),
        ],
        compiler_params=PARAMS,
        cost_estimate=cost(mm, 7 << 20),
    )(me, toks, gp)
    note = shift(dws[0, 0, :16], "c", 1)
    dws = lax.all_to_all(dws, "x", 0, 0, tiled=True)

    dx_own, *dx_other = pl.pallas_call(
        dx_kernel,
        out_shape=[jax.ShapeDtypeStruct((512, D), BF)] + [jax.ShapeDtypeStruct((256, D), BF)] * 2,
        in_specs=[SM, VM] + [ANY] * 2,
        out_specs=[VM] * 3,
        scratch_shapes=[pltpu.VMEM((D, FD), BF), pltpu.SemaphoreType.DMA((32,))],
        compiler_params=PARAMS,
        cost_estimate=cost(mm, 7 << 20),
    )(me, gp, wins, note)

    swapped = jnp.concatenate([shift(part, "c", 1) for part in dx_other])
    dx_c = add_up([dx_own, swapped]).astype(BF)
    dx_y = lax.all_to_all(dx_c, "y", 0, 0, tiled=True).reshape(4, TD, D)
    dwin_x = add_up([dws[i] for i in range(4)]).astype(BF)
    pairs = [dwin_x[2 * i : 2 * i + 2] for i in range(4)]
    moved = [shift(pairs[i], Z, r) for i, r in ((1, 1), (2, -1), (3, 2))]
    sent = [shift(dwo_z[i], "x", X_STEPS[i]) for i in range(1, 4)]
    *sent, m0, m1, m2 = lax.optimization_barrier((*sent, *moved))
    moved = [m0, m1, m2]
    dwin_z = add_up([pairs[0]] + moved).astype(BF)
    dwo_sum = add_up([dwo_z[0]] + sent).astype(BF)
    sums = jnp.stack([dwin_z[0], dwo_sum])
    near, far = turn(sums), turn(dwin_z[1], 1)
    grad_w_in = add_up([near[0], far])
    grad_w_out = near[1].astype(F32).T

    grad_in = pl.pallas_call(
        final_kernel,
        out_shape=jax.ShapeDtypeStruct((TD, D), BF),
        in_specs=[VM] * 4 + [ANY],
        out_specs=VM,
        compiler_params=PARAMS,
        cost_estimate=cost(20 * TD * D, 14 * TD * D),
    )(inputs, norm_gain, grad_out, dx_y, sums)
    return grad_in, grad_w_in, grad_w_out


def solution(mesh):
    fine = Mesh(mesh.devices.reshape(4, 2, 4, 4, 2), ("y", "zh", "x", "zl", "c"))
    dp, tensor = ("y", "zh", "x"), ("zl", "c")
    rows = P(dp + tensor, None)
    return jax.shard_map(
        on_device,
        mesh=fine,
        in_specs=(rows, P(), P(), P(dp, tensor), P(tensor), P(tensor, dp), rows),
        out_specs=(rows, P(dp, tensor), P(tensor, dp)),
        check_vma=False,
    )
```

```python
import functools

import jax
import jax.numpy as jnp
from jax import lax
from jax.experimental import pallas as pl
from jax.experimental.pallas import tpu as pltpu
from jax.sharding import Mesh, PartitionSpec as P

D = 1536
FD = 768
TD = 128
RB = 48
BF = jnp.bfloat16
F32 = jnp.float32
Z = ("zh", "zl")
X_STEPS = (0, 1, -1, 2)
Z_STEPS = tuple((r, h) for r in (0, 1, -1, 2) for h in (0, 4))
RING = tuple((k, (0, 1, 2, 3)) for k in (0, -1, 1, -2, 2, -3, 3)) + ((-4, (0, 1)), (4, (2, 3)))
SIZES = {"y": 4, "x": 4, "c": 2, Z: 8}
ANY = pl.BlockSpec(memory_space=pl.ANY)
VM = pl.BlockSpec(memory_space=pltpu.VMEM)
SM = pl.BlockSpec(memory_space=pltpu.SMEM)
PARAMS = pltpu.CompilerParams(vmem_limit_bytes=60 * 1024 * 1024)


def shift(value, axis, by):
    n = SIZES[axis]
    return lax.ppermute(value, axis, [(i, (i + by) % n) for i in range(n)])


def turn(value, far=0):
    pairs = [
        (y * 8 + h * 4 + z, z * 8 + (h ^ far) * 4 + y)
        for y in range(4)
        for h in range(2)
        for z in range(4)
    ]
    return lax.ppermute(value, ("y", "zh", "zl"), pairs)


def row_block(z, x):
    return ((z % 4) * 8 + (z // 4) * 4 + x) * RB


def rows_at(ref, z, x):
    return ref.at[pl.ds(pl.multiple_of(row_block(z, x), 16), RB)]


def norm_kernel(x_ref, gain_ref, bias_ref, grad_ref, out_ref):
    centred = x_ref[...].astype(F32)
    centred = centred - jnp.mean(centred, axis=-1, keepdims=True)
    variance = jnp.mean(centred * centred, axis=-1, keepdims=True)
    normed = centred * lax.rsqrt(variance + 1e-05)
    out_ref[0] = (normed * gain_ref[...] + bias_ref[...]).astype(BF)
    out_ref[1] = grad_ref[...]


def token_copies(toks, me, kind, dst, sems):
    copies = []
    for i in range(8):
        owner = (i % 4) * 2 + (me[2] if i < 4 else 1 - me[2])
        at = dst.at[pl.ds(i * TD, TD)]
        copies.append(pltpu.make_async_copy(toks.at[owner, kind], at, sems.at[i]))
    return copies


def win_copies(pieces, me, dst, sems):
    copies = []
    for i in range(4):
        for j, (r, h) in enumerate(Z_STEPS):
            at = rows_at(dst, (me[1] - r + h + 8) % 8, i)
            copies.append(pltpu.make_async_copy(pieces.at[i, j], at, sems.at[i * 8 + j]))
    return copies


def main_kernel(me, *refs):
    toks, wins, wos = refs[0], refs[1], refs[2:11]
    bias_ref, gp_ref, dwo_ref = refs[11:14]
    n_s, g_s, win_s, wo_s, act_s, dwo_s, sem_n, sem_g, sem_i, sem_o = refs[14:]
    n_copies = token_copies(toks, me, 0, n_s, sem_n)
    g_copies = token_copies(toks, me, 1, g_s, sem_g)
    i_copies = win_copies(wins, me, win_s, sem_i)
    o_copies = []
    for piece, (away, xs) in zip(wos, RING):
        for k, i in enumerate(xs):
            at = rows_at(wo_s, (me[1] + away + 8) % 8, (me[0] - X_STEPS[i] + 4) % 4)
            o_copies.append(pltpu.make_async_copy(piece.at[k], at, sem_o.at[len(o_copies)]))
    for copy in n_copies + i_copies + g_copies + o_copies:
        copy.start()
    for copy in n_copies + i_copies + g_copies + o_copies:
        copy.wait()

    pre = jnp.dot(n_s[...], win_s[...], preferred_element_type=F32) + bias_ref[...]
    ga = 0.5 * jnp.dot(g_s[...], wo_s[...], preferred_element_type=F32)
    s = jax.nn.sigmoid(pre)
    act_s[...] = (pre * s).astype(BF)
    gp_ref[...] = (ga * s * (1.0 + pre * (1.0 - s))).astype(BF)
    dims = (((0,), (0,)), ((), ()))

    def out_grad(half, carry):
        rows = pl.ds(pl.multiple_of(half * 768, 768), 768)
        dwo = lax.dot_general(g_s[:, rows], act_s[...], dims, preferred_element_type=F32)
        dwo_s[rows, :] = (0.5 * dwo).astype(BF)
        for zl, zh in ((half * 2, 0), (half * 2, 1), (half * 2 + 1, 0), (half * 2 + 1, 1)):
            for i, xs in enumerate(X_STEPS):
                src = rows_at(dwo_s, zh * 4 + zl, (me[0] + xs + 4) % 4)
                dst = dwo_ref.at[zh * 4 + zl, i]
                pltpu.make_async_copy(src, dst, sem_o.at[zl * 8 + zh * 4 + i]).start()
        return carry

    lax.fori_loop(0, 2, out_grad, 0)
    for k in range(32):
        pltpu.make_async_copy(dwo_s.at[pl.ds(0, RB)], dwo_ref.at[0, 0], sem_o.at[k]).wait()


def dwin_kernel(me, *refs):
    toks, gp_ref, dwin_ref, n_s, dwin_s, sem_n, sem_i = refs
    copies = token_copies(toks, me, 0, n_s, sem_n)
    for copy in copies:
        copy.start()
    for copy in copies:
        copy.wait()

    def in_grad(half, carry):
        rows = pl.ds(pl.multiple_of(half * 768, 768), 768)
        dims = (((0,), (0,)), ((), ()))
        dwin = lax.dot_general(n_s[:, rows], gp_ref[...], dims, preferred_element_type=F32)
        dwin_s[rows, :] = dwin.astype(BF)
        for zl, zh in ((half * 2, 0), (half * 2, 1), (half * 2 + 1, 0), (half * 2 + 1, 1)):
            away = (zh * 4 + zl - me[1] + 8) % 8
            quarter = away % 4
            place = 2 * (quarter ^ (quarter // 2)) + ((away + 1) // 4) % 2
            for x in range(4):
                src = rows_at(dwin_s, zh * 4 + zl, x)
                dst = dwin_ref.at[x, place]
                pltpu.make_async_copy(src, dst, sem_i.at[zl * 8 + zh * 4 + x]).start()
        return carry

    lax.fori_loop(0, 2, in_grad, 0)
    for k in range(32):
        pltpu.make_async_copy(dwin_s.at[pl.ds(0, RB)], dwin_ref.at[0, 0], sem_i.at[k]).wait()


def dx_kernel(me, *refs):
    gp_ref, wins, outs = refs[0], refs[1], refs[3:6]
    win_s, sem_i = refs[6:]
    copies = win_copies(wins, me, win_s, sem_i)
    for copy in copies:
        copy.start()
    for copy in copies:
        copy.wait()

    def step(j, carry):
        cols = pl.ds(pl.multiple_of(j * 768, 768), 768)
        dx = lax.dot_general(
            gp_ref[...], win_s[cols, :], (((1,), (1,)), ((), ())), preferred_element_type=F32
        ).astype(BF)
        outs[0][:, cols] = dx[:512]
        for i in range(2):
            outs[1 + i][:, cols] = dx[512 + 256 * i : 512 + 256 * (i + 1)]
        return carry

    lax.fori_loop(0, 2, step, 0)


def final_kernel(x_ref, gain_ref, grad_ref, dx_ref, after_ref, out_ref):
    centred = x_ref[...].astype(F32)
    centred = centred - jnp.mean(centred, axis=-1, keepdims=True)
    variance = jnp.mean(centred * centred, axis=-1, keepdims=True)
    inv_scale = lax.rsqrt(variance + 1e-05)
    normed = centred * inv_scale
    total = add_up([dx_ref[i] for i in range(4)])
    scaled = total * gain_ref[...]
    first = jnp.mean(scaled, axis=-1, keepdims=True)
    second = jnp.mean(scaled * normed, axis=-1, keepdims=True)
    result = grad_ref[...].astype(F32) + inv_scale * (scaled - first - normed * second)
    out_ref[...] = result.astype(BF)


def cost(flops, moved):
    return pl.CostEstimate(flops=flops, bytes_accessed=moved, transcendentals=0)


def add_up(parts):
    total = parts[0].astype(F32)
    for part in parts[1:]:
        total = total + part.astype(F32)
    return total


def on_device(inputs, norm_gain, norm_bias, w_in, bias_in, w_out, grad_out):
    me = jnp.stack([lax.axis_index(a) for a in ("x", Z, "c")]).astype(jnp.int32)

    both = turn(jnp.stack([w_in, w_out.T]))
    win_far = turn(w_in, 1)
    bias = turn(bias_in)

    tok = pl.pallas_call(
        norm_kernel,
        out_shape=jax.ShapeDtypeStruct((2, TD, D), BF),
        in_specs=[VM] * 4,
        out_specs=VM,
        compiler_params=PARAMS,
        cost_estimate=cost(10 * TD * D, 8 * TD * D),
    )(inputs, norm_gain, norm_bias, grad_out)

    me, bias, both, win_far, tok = lax.optimization_barrier((me, bias, both, win_far, tok))
    toks = lax.all_gather(tok, ("y", "c"), axis=0, tiled=False)

    wo_x = [both[1]] + [shift(both[1], "x", s) for s in X_STEPS[1:]]
    win_h = jnp.stack([both[0], win_far])
    win_z = [win_h] + [shift(win_h, Z, r) for r in (1, -1, 2)]
    *wo_x, w0, w1, w2, w3 = lax.optimization_barrier((*wo_x, *win_z))
    win_z = [w0, w1, w2, w3]
    wo_h = jnp.stack(wo_x)
    ahead, back = shift(wo_h, Z, 1), shift(wo_h, Z, -1)
    win_z = jnp.broadcast_to(jnp.concatenate(win_z)[None], (4, 8, RB, FD))
    wins = lax.all_to_all(win_z, "x", 0, 0, tiled=True)
    wos = [wo_h, ahead, back]
    for _ in range(2):
        ahead, back = shift(ahead, Z, 1), shift(back, Z, -1)
        wos += [ahead, back]
    wos += [shift(ahead[:2], Z, 1), shift(back[2:], Z, -1)]
    bias = bias.reshape(1, FD)

    mm = 2 * 1024 * FD * D
    gp, dwo = pl.pallas_call(
        main_kernel,
        out_shape=(
            jax.ShapeDtypeStruct((1024, FD), BF),
            jax.ShapeDtypeStruct((8, 4, RB, FD), BF),
        ),
        in_specs=[SM] + [ANY] * 11 + [VM],
        out_specs=(VM, ANY),
        scratch_shapes=[
            pltpu.VMEM((1024, D), BF),
            pltpu.VMEM((1024, D), BF),
            pltpu.VMEM((D, FD), BF),
            pltpu.VMEM((D, FD), BF),
            pltpu.VMEM((1024, FD), BF),
            pltpu.VMEM((D, FD), BF),
            pltpu.SemaphoreType.DMA((8,)),
            pltpu.SemaphoreType.DMA((8,)),
            pltpu.SemaphoreType.DMA((32,)),
            pltpu.SemaphoreType.DMA((32,)),
        ],
        compiler_params=PARAMS,
        cost_estimate=cost(3 * mm, 20 << 20),
    )(me, toks, wins, *wos, bias)

    dwo_z = lax.psum_scatter(dwo, Z, scatter_dimension=0, tiled=False)

    dws = pl.pallas_call(
        dwin_kernel,
        out_shape=jax.ShapeDtypeStruct((4, 8, RB, FD), BF),
        in_specs=[SM, ANY, VM],
        out_specs=ANY,
        scratch_shapes=[
            pltpu.VMEM((1024, D), BF),
            pltpu.VMEM((D, FD), BF),
            pltpu.SemaphoreType.DMA((8,)),
            pltpu.SemaphoreType.DMA((32,)),
        ],
        compiler_params=PARAMS,
        cost_estimate=cost(mm, 7 << 20),
    )(me, toks, gp)
    note = dws
    dws = lax.all_to_all(dws, "x", 0, 0, tiled=True)

    dx_own, *dx_other = pl.pallas_call(
        dx_kernel,
        out_shape=[jax.ShapeDtypeStruct((512, D), BF)] + [jax.ShapeDtypeStruct((256, D), BF)] * 2,
        in_specs=[SM, VM] + [ANY] * 2,
        out_specs=[VM] * 3,
        scratch_shapes=[pltpu.VMEM((D, FD), BF), pltpu.SemaphoreType.DMA((32,))],
        compiler_params=PARAMS,
        cost_estimate=cost(mm, 7 << 20),
    )(me, gp, wins, note)

    swapped = jnp.concatenate([shift(part, "c", 1) for part in dx_other])
    dx_c = add_up([dx_own, swapped]).astype(BF)
    dx_y = lax.all_to_all(dx_c, "y", 0, 0, tiled=True).reshape(4, TD, D)
    dwin_x = add_up([dws[i] for i in range(4)]).astype(BF)
    pairs = [dwin_x[2 * i : 2 * i + 2] for i in range(4)]
    moved = [shift(pairs[i], Z, r) for i, r in ((1, 1), (2, -1), (3, 2))]
    sent = [shift(dwo_z[i], "x", X_STEPS[i]) for i in range(1, 4)]
    *sent, m0, m1, m2 = lax.optimization_barrier((*sent, *moved))
    moved = [m0, m1, m2]
    dwin_z = add_up([pairs[0]] + moved).astype(BF)
    dwo_sum = add_up([dwo_z[0]] + sent).astype(BF)
    sums = jnp.stack([dwin_z[0], dwo_sum])
    near, far = turn(sums), turn(dwin_z[1], 1)
    grad_w_in = add_up([near[0], far])
    grad_w_out = near[1].astype(F32).T

    grad_in = pl.pallas_call(
        final_kernel,
        out_shape=jax.ShapeDtypeStruct((TD, D), BF),
        in_specs=[VM] * 4 + [ANY],
        out_specs=VM,
        compiler_params=PARAMS,
        cost_estimate=cost(20 * TD * D, 14 * TD * D),
    )(inputs, norm_gain, grad_out, dx_y, sums)
    return grad_in, grad_w_in, grad_w_out


def solution(mesh):
    fine = Mesh(mesh.devices.reshape(4, 2, 4, 4, 2), ("y", "zh", "x", "zl", "c"))
    dp, tensor = ("y", "zh", "x"), ("zl", "c")
    rows = P(dp + tensor, None)
    return jax.shard_map(
        on_device,
        mesh=fine,
        in_specs=(rows, P(), P(), P(dp, tensor), P(tensor), P(tensor, dp), rows),
        out_specs=(rows, P(dp, tensor), P(tensor, dp)),
        check_vma=False,
    )
```

```python
import functools

import jax
import jax.numpy as jnp
from jax import lax
from jax.experimental import pallas as pl
from jax.experimental.pallas import tpu as pltpu
from jax.sharding import Mesh, PartitionSpec as P

D = 1536
FD = 768
TD = 128
RB = 48
BF = jnp.bfloat16
F32 = jnp.float32
Z = ("zh", "zl")
X_STEPS = (0, 1, -1, 2)
Z_STEPS = tuple((r, h) for r in (0, 1, -1, 2) for h in (0, 4))
RING = tuple((k, (0, 1, 2, 3)) for k in (0, -1, 1)) + ((-2, (0, 1)), (2, (2, 3)))
SIZES = {"y": 4, "x": 4, "c": 2, Z: 8}
ANY = pl.BlockSpec(memory_space=pl.ANY)
VM = pl.BlockSpec(memory_space=pltpu.VMEM)
SM = pl.BlockSpec(memory_space=pltpu.SMEM)
PARAMS = pltpu.CompilerParams(vmem_limit_bytes=60 * 1024 * 1024)


def shift(value, axis, by):
    n = SIZES[axis]
    return lax.ppermute(value, axis, [(i, (i + by) % n) for i in range(n)])


def turn(value, far=0):
    pairs = [
        (y * 8 + h * 4 + z, z * 8 + (h ^ far) * 4 + y)
        for y in range(4)
        for h in range(2)
        for z in range(4)
    ]
    return lax.ppermute(value, ("y", "zh", "zl"), pairs)


def row_block(z, x):
    return ((z % 4) * 8 + (z // 4) * 4 + x) * RB


def rows_at(ref, z, x):
    return ref.at[pl.ds(pl.multiple_of(row_block(z, x), 16), RB)]


def norm_kernel(x_ref, gain_ref, bias_ref, grad_ref, out_ref):
    centred = x_ref[...].astype(F32)
    centred = centred - jnp.mean(centred, axis=-1, keepdims=True)
    variance = jnp.mean(centred * centred, axis=-1, keepdims=True)
    normed = centred * lax.rsqrt(variance + 1e-05)
    out_ref[0] = (normed * gain_ref[...] + bias_ref[...]).astype(BF)
    out_ref[1] = grad_ref[...]


def token_copies(toks, me, kind, dst, sems):
    copies = []
    for i in range(8):
        owner = (i % 4) * 2 + (me[2] if i < 4 else 1 - me[2])
        at = dst.at[pl.ds(i * TD, TD)]
        copies.append(pltpu.make_async_copy(toks.at[owner, kind], at, sems.at[i]))
    return copies


def win_copies(pieces, me, dst, sems):
    copies = []
    for i in range(4):
        for j, (r, h) in enumerate(Z_STEPS):
            at = rows_at(dst, (me[1] - r + h + 8) % 8, i)
            copies.append(pltpu.make_async_copy(pieces.at[i, j], at, sems.at[i * 8 + j]))
    return copies


def main_kernel(me, *refs):
    toks, wins, wos = refs[0], refs[1], refs[2:7]
    bias_ref, gp_ref, dwo_ref = refs[7:10]
    n_s, g_s, win_s, wo_s, act_s, dwo_s, sem_n, sem_g, sem_i, sem_o = refs[10:]
    n_copies = token_copies(toks, me, 0, n_s, sem_n)
    g_copies = token_copies(toks, me, 1, g_s, sem_g)
    i_copies = win_copies(wins, me, win_s, sem_i)
    o_copies = []
    for piece, (away, xs) in zip(wos, RING):
        for k, i in enumerate(xs):
            for h in range(2):
                z = (me[1] + away + 4 * h + 8) % 8
                at = rows_at(wo_s, z, (me[0] - X_STEPS[i] + 4) % 4)
                o_copies.append(pltpu.make_async_copy(piece.at[k, h], at, sem_o.at[len(o_copies)]))
    for copy in n_copies + i_copies + g_copies + o_copies:
        copy.start()
    for copy in n_copies + i_copies + g_copies + o_copies:
        copy.wait()

    pre = jnp.dot(n_s[...], win_s[...], preferred_element_type=F32) + bias_ref[...]
    ga = 0.5 * jnp.dot(g_s[...], wo_s[...], preferred_element_type=F32)
    s = jax.nn.sigmoid(pre)
    act_s[...] = (pre * s).astype(BF)
    gp_ref[...] = (ga * s * (1.0 + pre * (1.0 - s))).astype(BF)
    dims = (((0,), (0,)), ((), ()))

    def out_grad(half, carry):
        rows = pl.ds(pl.multiple_of(half * 768, 768), 768)
        dwo = lax.dot_general(g_s[:, rows], act_s[...], dims, preferred_element_type=F32)
        dwo_s[rows, :] = (0.5 * dwo).astype(BF)
        for zl, zh in ((half * 2, 0), (half * 2, 1), (half * 2 + 1, 0), (half * 2 + 1, 1)):
            for i, xs in enumerate(X_STEPS):
                src = rows_at(dwo_s, zh * 4 + zl, (me[0] + xs + 4) % 4)
                dst = dwo_ref.at[zh * 4 + zl, i]
                pltpu.make_async_copy(src, dst, sem_o.at[zl * 8 + zh * 4 + i]).start()
        return carry

    lax.fori_loop(0, 2, out_grad, 0)
    for k in range(32):
        pltpu.make_async_copy(dwo_s.at[pl.ds(0, RB)], dwo_ref.at[0, 0], sem_o.at[k]).wait()


def dwin_kernel(me, *refs):
    toks, gp_ref, dwin_ref, n_s, dwin_s, sem_n, sem_i = refs
    copies = token_copies(toks, me, 0, n_s, sem_n)
    for copy in copies:
        copy.start()
    for copy in copies:
        copy.wait()

    def in_grad(half, carry):
        rows = pl.ds(pl.multiple_of(half * 768, 768), 768)
        dims = (((0,), (0,)), ((), ()))
        dwin = lax.dot_general(n_s[:, rows], gp_ref[...], dims, preferred_element_type=F32)
        dwin_s[rows, :] = dwin.astype(BF)
        for zl, zh in ((half * 2, 0), (half * 2, 1), (half * 2 + 1, 0), (half * 2 + 1, 1)):
            away = (zh * 4 + zl - me[1] + 8) % 8
            quarter = away % 4
            place = 2 * (quarter ^ (quarter // 2)) + ((away + 1) // 4) % 2
            for x in range(4):
                src = rows_at(dwin_s, zh * 4 + zl, x)
                dst = dwin_ref.at[x, place]
                pltpu.make_async_copy(src, dst, sem_i.at[zl * 8 + zh * 4 + x]).start()
        return carry

    lax.fori_loop(0, 2, in_grad, 0)
    for k in range(32):
        pltpu.make_async_copy(dwin_s.at[pl.ds(0, RB)], dwin_ref.at[0, 0], sem_i.at[k]).wait()


def dx_kernel(me, *refs):
    gp_ref, wins, outs = refs[0], refs[1], refs[3:6]
    win_s, sem_i = refs[6:]
    copies = win_copies(wins, me, win_s, sem_i)
    for copy in copies:
        copy.start()
    for copy in copies:
        copy.wait()

    def step(j, carry):
        cols = pl.ds(pl.multiple_of(j * 768, 768), 768)
        dx = lax.dot_general(
            gp_ref[...], win_s[cols, :], (((1,), (1,)), ((), ())), preferred_element_type=F32
        ).astype(BF)
        outs[0][:, cols] = dx[:512]
        for i in range(2):
            outs[1 + i][:, cols] = dx[512 + 256 * i : 512 + 256 * (i + 1)]
        return carry

    lax.fori_loop(0, 2, step, 0)


def final_kernel(x_ref, gain_ref, grad_ref, dx_ref, after_ref, out_ref):
    centred = x_ref[...].astype(F32)
    centred = centred - jnp.mean(centred, axis=-1, keepdims=True)
    variance = jnp.mean(centred * centred, axis=-1, keepdims=True)
    inv_scale = lax.rsqrt(variance + 1e-05)
    normed = centred * inv_scale
    total = add_up([dx_ref[i] for i in range(4)])
    scaled = total * gain_ref[...]
    first = jnp.mean(scaled, axis=-1, keepdims=True)
    second = jnp.mean(scaled * normed, axis=-1, keepdims=True)
    result = grad_ref[...].astype(F32) + inv_scale * (scaled - first - normed * second)
    out_ref[...] = result.astype(BF)


def cost(flops, moved):
    return pl.CostEstimate(flops=flops, bytes_accessed=moved, transcendentals=0)


def add_up(parts):
    total = parts[0].astype(F32)
    for part in parts[1:]:
        total = total + part.astype(F32)
    return total


def on_device(inputs, norm_gain, norm_bias, w_in, bias_in, w_out, grad_out):
    me = jnp.stack([lax.axis_index(a) for a in ("x", Z, "c")]).astype(jnp.int32)

    weights = jnp.stack([w_in, w_out.T])
    both, far_both = turn(weights), turn(weights, 1)
    bias = turn(bias_in)

    tok = pl.pallas_call(
        norm_kernel,
        out_shape=jax.ShapeDtypeStruct((2, TD, D), BF),
        in_specs=[VM] * 4,
        out_specs=VM,
        compiler_params=PARAMS,
        cost_estimate=cost(10 * TD * D, 8 * TD * D),
    )(inputs, norm_gain, norm_bias, grad_out)

    me, bias, both, far_both, tok = lax.optimization_barrier((me, bias, both, far_both, tok))
    toks = lax.all_gather(tok, ("y", "c"), axis=0, tiled=False)

    wo_pair = jnp.stack([both[1], far_both[1]])
    wo_x = [wo_pair] + [shift(wo_pair, "x", s) for s in X_STEPS[1:]]
    win_h = jnp.stack([both[0], far_both[0]])
    win_z = [win_h] + [shift(win_h, Z, r) for r in (1, -1, 2)]
    *wo_x, w0, w1, w2, w3 = lax.optimization_barrier((*wo_x, *win_z))
    win_z = [w0, w1, w2, w3]
    wo_h = jnp.stack(wo_x)
    ahead, back = shift(wo_h, Z, 1), shift(wo_h, Z, -1)
    win_z = jnp.broadcast_to(jnp.concatenate(win_z)[None], (4, 8, RB, FD))
    wins = lax.all_to_all(win_z, "x", 0, 0, tiled=True)
    wos = [wo_h, ahead, back]
    wos += [shift(ahead[:2], Z, 1), shift(back[2:], Z, -1)]
    bias = bias.reshape(1, FD)

    mm = 2 * 1024 * FD * D
    gp, dwo = pl.pallas_call(
        main_kernel,
        out_shape=(
            jax.ShapeDtypeStruct((1024, FD), BF),
            jax.ShapeDtypeStruct((8, 4, RB, FD), BF),
        ),
        in_specs=[SM] + [ANY] * 7 + [VM],
        out_specs=(VM, ANY),
        scratch_shapes=[
            pltpu.VMEM((1024, D), BF),
            pltpu.VMEM((1024, D), BF),
            pltpu.VMEM((D, FD), BF),
            pltpu.VMEM((D, FD), BF),
            pltpu.VMEM((1024, FD), BF),
            pltpu.VMEM((D, FD), BF),
            pltpu.SemaphoreType.DMA((8,)),
            pltpu.SemaphoreType.DMA((8,)),
            pltpu.SemaphoreType.DMA((32,)),
            pltpu.SemaphoreType.DMA((32,)),
        ],
        compiler_params=PARAMS,
        cost_estimate=cost(3 * mm, 20 << 20),
    )(me, toks, wins, *wos, bias)

    dwo_z = lax.psum_scatter(dwo, Z, scatter_dimension=0, tiled=False)

    dws = pl.pallas_call(
        dwin_kernel,
        out_shape=jax.ShapeDtypeStruct((4, 8, RB, FD), BF),
        in_specs=[SM, ANY, VM],
        out_specs=ANY,
        scratch_shapes=[
            pltpu.VMEM((1024, D), BF),
            pltpu.VMEM((D, FD), BF),
            pltpu.SemaphoreType.DMA((8,)),
            pltpu.SemaphoreType.DMA((32,)),
        ],
        compiler_params=PARAMS,
        cost_estimate=cost(mm, 7 << 20),
    )(me, toks, gp)
    note = dws
    dws = lax.all_to_all(dws, "x", 0, 0, tiled=True)

    dx_own, *dx_other = pl.pallas_call(
        dx_kernel,
        out_shape=[jax.ShapeDtypeStruct((512, D), BF)] + [jax.ShapeDtypeStruct((256, D), BF)] * 2,
        in_specs=[SM, VM] + [ANY] * 2,
        out_specs=[VM] * 3,
        scratch_shapes=[pltpu.VMEM((D, FD), BF), pltpu.SemaphoreType.DMA((32,))],
        compiler_params=PARAMS,
        cost_estimate=cost(mm, 7 << 20),
    )(me, gp, wins, note)

    swapped = jnp.concatenate([shift(part, "c", 1) for part in dx_other])
    dx_c = add_up([dx_own, swapped]).astype(BF)
    dx_y = lax.all_to_all(dx_c, "y", 0, 0, tiled=True).reshape(4, TD, D)
    dwin_x = add_up([dws[i] for i in range(4)]).astype(BF)
    pairs = [dwin_x[2 * i : 2 * i + 2] for i in range(4)]
    moved = [shift(pairs[i], Z, r) for i, r in ((1, 1), (2, -1), (3, 2))]
    sent = [shift(dwo_z[i], "x", X_STEPS[i]) for i in range(1, 4)]
    *sent, m0, m1, m2 = lax.optimization_barrier((*sent, *moved))
    moved = [m0, m1, m2]
    dwin_z = add_up([pairs[0]] + moved).astype(BF)
    dwo_sum = add_up([dwo_z[0]] + sent).astype(BF)
    sums = jnp.stack([dwin_z[0], dwo_sum])
    near, far = turn(sums), turn(dwin_z[1], 1)
    grad_w_in = add_up([near[0], far])
    grad_w_out = near[1].astype(F32).T

    grad_in = pl.pallas_call(
        final_kernel,
        out_shape=jax.ShapeDtypeStruct((TD, D), BF),
        in_specs=[VM] * 4 + [ANY],
        out_specs=VM,
        compiler_params=PARAMS,
        cost_estimate=cost(20 * TD * D, 14 * TD * D),
    )(inputs, norm_gain, grad_out, dx_y, sums)
    return grad_in, grad_w_in, grad_w_out


def solution(mesh):
    fine = Mesh(mesh.devices.reshape(4, 2, 4, 4, 2), ("y", "zh", "x", "zl", "c"))
    dp, tensor = ("y", "zh", "x"), ("zl", "c")
    rows = P(dp + tensor, None)
    return jax.shard_map(
        on_device,
        mesh=fine,
        in_specs=(rows, P(), P(), P(dp, tensor), P(tensor), P(tensor, dp), rows),
        out_specs=(rows, P(dp, tensor), P(tensor, dp)),
        check_vma=False,
    )
```

```python
import functools

import jax
import jax.numpy as jnp
from jax import lax
from jax.experimental import pallas as pl
from jax.experimental.pallas import tpu as pltpu
from jax.sharding import Mesh, PartitionSpec as P

D = 1536
FD = 768
TD = 128
RB = 48
BF = jnp.bfloat16
F32 = jnp.float32
Z = ("zh", "zl")
X_STEPS = (0, 1, -1, 2)
Z_STEPS = tuple((r, h) for r in (0, 1, -1, 2) for h in (0, 4))
RING = tuple((k, (0, 1, 2, 3)) for k in (0, -1, 1, -2, 2, -3, 3)) + ((-4, (0, 1)), (4, (2, 3)))
SIZES = {"y": 4, "x": 4, "c": 2, Z: 8}
ANY = pl.BlockSpec(memory_space=pl.ANY)
VM = pl.BlockSpec(memory_space=pltpu.VMEM)
SM = pl.BlockSpec(memory_space=pltpu.SMEM)
PARAMS = pltpu.CompilerParams(vmem_limit_bytes=60 * 1024 * 1024)


def shift(value, axis, by):
    n = SIZES[axis]
    return lax.ppermute(value, axis, [(i, (i + by) % n) for i in range(n)])


def turn(value, far=0):
    pairs = [
        (y * 8 + h * 4 + z, z * 8 + (h ^ far) * 4 + y)
        for y in range(4)
        for h in range(2)
        for z in range(4)
    ]
    return lax.ppermute(value, ("y", "zh", "zl"), pairs)


def row_block(z, x):
    return ((z % 4) * 8 + (z // 4) * 4 + x) * RB


def rows_at(ref, z, x):
    return ref.at[pl.ds(pl.multiple_of(row_block(z, x), 16), RB)]


def norm_kernel(x_ref, gain_ref, bias_ref, grad_ref, out_ref):
    centred = x_ref[...].astype(F32)
    centred = centred - jnp.mean(centred, axis=-1, keepdims=True)
    variance = jnp.mean(centred * centred, axis=-1, keepdims=True)
    normed = centred * lax.rsqrt(variance + 1e-05)
    out_ref[0] = (normed * gain_ref[...] + bias_ref[...]).astype(BF)
    out_ref[1] = grad_ref[...]


def token_copies(toks, me, kind, dst, sems):
    copies = []
    for i in range(8):
        owner = (i % 4) * 2 + (me[2] if i < 4 else 1 - me[2])
        at = dst.at[pl.ds(i * TD, TD)]
        copies.append(pltpu.make_async_copy(toks.at[owner, kind], at, sems.at[i]))
    return copies


def win_copies(pieces, me, dst, sems):
    copies = []
    for i in range(4):
        for j, (r, h) in enumerate(Z_STEPS):
            at = rows_at(dst, (me[1] - r + h + 8) % 8, i)
            copies.append(pltpu.make_async_copy(pieces.at[i, j], at, sems.at[i * 8 + j]))
    return copies


def main_kernel(me, *refs):
    toks, wins, wos = refs[0], refs[1], refs[2:11]
    bias_ref, gp_ref, dwo_ref = refs[11:14]
    n_s, g_s, win_s, wo_s, act_s, dwo_s, sem_n, sem_g, sem_i, sem_o = refs[14:]
    n_copies = token_copies(toks, me, 0, n_s, sem_n)
    g_copies = token_copies(toks, me, 1, g_s, sem_g)
    i_copies = win_copies(wins, me, win_s, sem_i)
    o_copies = []
    for piece, (away, xs) in zip(wos, RING):
        for k, i in enumerate(xs):
            at = rows_at(wo_s, (me[1] + away + 8) % 8, (me[0] - X_STEPS[i] + 4) % 4)
            o_copies.append(pltpu.make_async_copy(piece.at[k], at, sem_o.at[len(o_copies)]))
    for copy in n_copies + i_copies + g_copies + o_copies:
        copy.start()
    for copy in n_copies + i_copies + g_copies + o_copies:
        copy.wait()

    pre = jnp.dot(n_s[...], win_s[...], preferred_element_type=F32) + bias_ref[...]
    ga = 0.5 * jnp.dot(g_s[...], wo_s[...], preferred_element_type=F32)
    s = jax.nn.sigmoid(pre)
    act_s[...] = (pre * s).astype(BF)
    gp_ref[...] = (ga * s * (1.0 + pre * (1.0 - s))).astype(BF)
    dims = (((0,), (0,)), ((), ()))

    def out_grad(half, carry):
        rows = pl.ds(pl.multiple_of(half * 768, 768), 768)
        dwo = lax.dot_general(g_s[:, rows], act_s[...], dims, preferred_element_type=F32)
        dwo_s[rows, :] = (0.5 * dwo).astype(BF)
        for zl, zh in ((half * 2, 0), (half * 2, 1), (half * 2 + 1, 0), (half * 2 + 1, 1)):
            for i, xs in enumerate(X_STEPS):
                src = rows_at(dwo_s, zh * 4 + zl, (me[0] + xs + 4) % 4)
                dst = dwo_ref.at[zh * 4 + zl, i]
                pltpu.make_async_copy(src, dst, sem_o.at[zl * 8 + zh * 4 + i]).start()
        return carry

    lax.fori_loop(0, 2, out_grad, 0)
    for k in range(32):
        pltpu.make_async_copy(dwo_s.at[pl.ds(0, RB)], dwo_ref.at[0, 0], sem_o.at[k]).wait()


def dwin_kernel(me, *refs):
    toks, gp_ref, dwin_ref, n_s, dwin_s, sem_n, sem_i = refs
    copies = token_copies(toks, me, 0, n_s, sem_n)
    for copy in copies:
        copy.start()
    for copy in copies:
        copy.wait()

    def in_grad(half, carry):
        rows = pl.ds(pl.multiple_of(half * 768, 768), 768)
        dims = (((0,), (0,)), ((), ()))
        dwin = lax.dot_general(n_s[:, rows], gp_ref[...], dims, preferred_element_type=F32)
        dwin_s[rows, :] = dwin.astype(BF)
        for zl, zh in ((half * 2, 0), (half * 2, 1), (half * 2 + 1, 0), (half * 2 + 1, 1)):
            away = (zh * 4 + zl - me[1] + 8) % 8
            quarter = away % 4
            place = 2 * (quarter ^ (quarter // 2)) + ((away + 1) // 4) % 2
            for x in range(4):
                src = rows_at(dwin_s, zh * 4 + zl, x)
                dst = dwin_ref.at[x, place]
                pltpu.make_async_copy(src, dst, sem_i.at[zl * 8 + zh * 4 + x]).start()
        return carry

    lax.fori_loop(0, 2, in_grad, 0)
    for k in range(32):
        pltpu.make_async_copy(dwin_s.at[pl.ds(0, RB)], dwin_ref.at[0, 0], sem_i.at[k]).wait()


def dx_kernel(me, *refs):
    gp_ref, wins, outs = refs[0], refs[1], refs[3:6]
    win_s, sem_i = refs[6:]
    copies = win_copies(wins, me, win_s, sem_i)
    for copy in copies:
        copy.start()
    for copy in copies:
        copy.wait()

    def step(j, carry):
        cols = pl.ds(pl.multiple_of(j * 768, 768), 768)
        dx = lax.dot_general(
            gp_ref[...], win_s[cols, :], (((1,), (1,)), ((), ())), preferred_element_type=F32
        ).astype(BF)
        outs[0][:, cols] = dx[:512]
        for i in range(2):
            outs[1 + i][:, cols] = dx[512 + 256 * i : 512 + 256 * (i + 1)]
        return carry

    lax.fori_loop(0, 2, step, 0)


def final_kernel(x_ref, gain_ref, grad_ref, dx_ref, after_ref, out_ref):
    centred = x_ref[...].astype(F32)
    centred = centred - jnp.mean(centred, axis=-1, keepdims=True)
    variance = jnp.mean(centred * centred, axis=-1, keepdims=True)
    inv_scale = lax.rsqrt(variance + 1e-05)
    normed = centred * inv_scale
    total = add_up([dx_ref[i] for i in range(4)])
    scaled = total * gain_ref[...]
    first = jnp.mean(scaled, axis=-1, keepdims=True)
    second = jnp.mean(scaled * normed, axis=-1, keepdims=True)
    result = grad_ref[...].astype(F32) + inv_scale * (scaled - first - normed * second)
    out_ref[...] = result.astype(BF)


def cost(flops, moved):
    return pl.CostEstimate(flops=flops, bytes_accessed=moved, transcendentals=0)


def add_up(parts):
    total = parts[0].astype(F32)
    for part in parts[1:]:
        total = total + part.astype(F32)
    return total


def on_device(inputs, norm_gain, norm_bias, w_in, bias_in, w_out, grad_out):
    me = jnp.stack([lax.axis_index(a) for a in ("x", Z, "c")]).astype(jnp.int32)

    both = turn(jnp.stack([w_in, w_out.T]))
    win_far = turn(w_in, 1)
    bias = turn(bias_in)

    tok = pl.pallas_call(
        norm_kernel,
        out_shape=jax.ShapeDtypeStruct((2, TD, D), BF),
        in_specs=[VM] * 4,
        out_specs=VM,
        compiler_params=PARAMS,
        cost_estimate=cost(10 * TD * D, 8 * TD * D),
    )(inputs, norm_gain, norm_bias, grad_out)

    me, bias, both, win_far, tok = lax.optimization_barrier((me, bias, both, win_far, tok))
    toks = lax.all_gather(tok, ("y", "c"), axis=0, tiled=False)

    wo_x = [both[1]] + [shift(both[1], "x", s) for s in X_STEPS[1:]]
    win_h = jnp.stack([both[0], win_far])
    win_z = [win_h] + [shift(win_h, Z, r) for r in (1, -1, 2)]
    *wo_x, w0, w1, w2, w3 = lax.optimization_barrier((*wo_x, *win_z))
    win_z = [w0, w1, w2, w3]
    wo_h = jnp.stack(wo_x)
    ahead, back = shift(wo_h, Z, 1), shift(wo_h, Z, -1)
    win_z = jnp.broadcast_to(jnp.concatenate(win_z)[None], (4, 8, RB, FD))
    wins = lax.all_to_all(win_z, "x", 0, 0, tiled=True)
    wos = [wo_h, ahead, back]
    for _ in range(2):
        ahead, back = shift(ahead, Z, 1), shift(back, Z, -1)
        wos += [ahead, back]
    wos += [shift(ahead[:2], Z, 1), shift(back[2:], Z, -1)]
    bias = bias.reshape(1, FD)

    mm = 2 * 1024 * FD * D
    gp, dwo = pl.pallas_call(
        main_kernel,
        out_shape=(
            jax.ShapeDtypeStruct((1024, FD), BF),
            jax.ShapeDtypeStruct((8, 4, RB, FD), BF),
        ),
        in_specs=[SM] + [ANY] * 11 + [VM],
        out_specs=(VM, ANY),
        scratch_shapes=[
            pltpu.VMEM((1024, D), BF),
            pltpu.VMEM((1024, D), BF),
            pltpu.VMEM((D, FD), BF),
            pltpu.VMEM((D, FD), BF),
            pltpu.VMEM((1024, FD), BF),
            pltpu.VMEM((D, FD), BF),
            pltpu.SemaphoreType.DMA((8,)),
            pltpu.SemaphoreType.DMA((8,)),
            pltpu.SemaphoreType.DMA((32,)),
            pltpu.SemaphoreType.DMA((32,)),
        ],
        compiler_params=PARAMS,
        cost_estimate=cost(3 * mm, 20 << 20),
    )(me, toks, wins, *wos, bias)

    dwo_z = lax.psum_scatter(dwo, Z, scatter_dimension=0, tiled=False)

    dws = pl.pallas_call(
        dwin_kernel,
        out_shape=jax.ShapeDtypeStruct((4, 8, RB, FD), BF),
        in_specs=[SM, ANY, VM],
        out_specs=ANY,
        scratch_shapes=[
            pltpu.VMEM((1024, D), BF),
            pltpu.VMEM((D, FD), BF),
            pltpu.SemaphoreType.DMA((8,)),
            pltpu.SemaphoreType.DMA((32,)),
        ],
        compiler_params=PARAMS,
        cost_estimate=cost(mm, 7 << 20),
    )(me, toks, gp)
    note = dws
    dws = lax.all_to_all(dws, "x", 0, 0, tiled=True)

    dx_own, *dx_other = pl.pallas_call(
        dx_kernel,
        out_shape=[jax.ShapeDtypeStruct((512, D), BF)] + [jax.ShapeDtypeStruct((256, D), BF)] * 2,
        in_specs=[SM, VM] + [ANY] * 2,
        out_specs=[VM] * 3,
        scratch_shapes=[pltpu.VMEM((D, FD), BF), pltpu.SemaphoreType.DMA((32,))],
        compiler_params=PARAMS,
        cost_estimate=cost(mm, 7 << 20),
    )(me, gp, wins, note)

    swapped = jnp.concatenate([shift(part, "c", 1) for part in dx_other])
    dx_c = add_up([dx_own, swapped]).astype(BF)
    dx_y = lax.all_to_all(dx_c, "y", 0, 0, tiled=True).reshape(4, TD, D)
    dwin_x = add_up([dws[i] for i in range(4)]).astype(BF)
    pairs = [dwin_x[2 * i : 2 * i + 2] for i in range(4)]
    moved = [shift(pairs[i], Z, r) for i, r in ((1, 1), (2, -1), (3, 2))]
    sent = [shift(dwo_z[i], "x", X_STEPS[i]) for i in range(1, 4)]
    *sent, m0, m1, m2 = lax.optimization_barrier((*sent, *moved))
    moved = [m0, m1, m2]
    dwin_z = add_up([pairs[0]] + moved).astype(BF)
    dwo_sum = add_up([dwo_z[0]] + sent).astype(BF)
    sums = jnp.stack([dwin_z[0], dwo_sum])
    near, far = turn(sums), turn(dwin_z[1], 1)
    grad_w_in = add_up([near[0], far])
    grad_w_out = near[1].astype(F32).T

    grad_in = pl.pallas_call(
        final_kernel,
        out_shape=jax.ShapeDtypeStruct((TD, D), BF),
        in_specs=[VM] * 4 + [ANY],
        out_specs=VM,
        compiler_params=PARAMS,
        cost_estimate=cost(20 * TD * D, 14 * TD * D),
    )(inputs, norm_gain, grad_out, dx_y, far)
    return grad_in, grad_w_in, grad_w_out


def solution(mesh):
    fine = Mesh(mesh.devices.reshape(4, 2, 4, 4, 2), ("y", "zh", "x", "zl", "c"))
    dp, tensor = ("y", "zh", "x"), ("zl", "c")
    rows = P(dp + tensor, None)
    return jax.shard_map(
        on_device,
        mesh=fine,
        in_specs=(rows, P(), P(), P(dp, tensor), P(tensor), P(tensor, dp), rows),
        out_specs=(rows, P(dp, tensor), P(tensor, dp)),
        check_vma=False,
    )
```
